512 devices in a mesh: segment: 32 (over z, core), neuron: 16 (over y, x).
Axes of the slice: x: 4, y: 4, z: 16, core: 2. Of those that a mesh axis runs over, the one named last changes fastest.
Arguments:
- pending_minibatch: bfloat16 [32, 8, 65536], P('segment', None, 'neuron'), may hold values from 0 to 32
- arriving_minibatches: bfloat16 [1, 8, 65536], P(None, None, 'neuron'), may hold values from 0 to 32
- coefficient_tiles: bfloat16 [32, 2, 4, 64, 65536], P('segment', None, None, None, 'neuron'), may hold values from -0.375 to 0.375
- offset_vector: float32 [32, 2, 65536], P('segment', None, 'neuron'), may hold values from -4 to 2
- source_tile_lookup: int32 [32, 2, 4, 1024], P('segment', None, None, 'neuron'), may hold values from 0 to 1023, as said below
- depth_of_segment: int32 [32], P('segment'), may hold values from 1 to 2, as said below
Outputs:
- section_out: bfloat16 [32, 8, 65536], P('segment', None, 'neuron')
The draws below stay inside these ranges and needn't reach their ends.
Inputs may be any that keep to these rules, and one draw needn't show every extreme that they name: `depth_of_segment`: every section has at least one layer and some section has 2. `source_tile_lookup`: for each section, layer and group of 64 consecutive output blocks, the 256 entries name input blocks from each of the 16 groups of 64 consecutive input blocks exactly equally often.
All inputs are finite; a program needn't handle non-finite values.
Results may differ from the reference program's by a relative error of at most 0.0051.
Values may be sent and summed in bfloat16 or wider, within the bound.
A program may use at most 128 MiB of HBM per device.

```python
import jax
import jax.numpy as jnp
from jax import lax

UNITS_OF_LEVEL = 65536
BLK = 64
KB = 4
LMAX = 2
STEPS = 2
SMALL_BATCH_SIZE = 8
NB = 1024
N_SEGMENT = 32
N_NEURON = 16


def draw_depth_of_segment(key, part):
    key = jax.random.fold_in(key, 7)
    first, second, third = jax.random.split(key, 3)
    counts = jax.random.randint(first, (N_SEGMENT,), 1, LMAX + 1)
    where_most = jax.random.randint(second, (), 0, N_SEGMENT)
    counts = jnp.where(jnp.arange(N_SEGMENT) == where_most, LMAX, counts)
    where_least = jax.random.randint(third, (), 0, N_SEGMENT)
    counts = jnp.where((jnp.arange(N_SEGMENT) == where_least) & (where_least != where_most), 1, counts)
    return counts.astype(jnp.int32)


def draw_source_tile_lookup(key, part):
    key = jax.random.fold_in(key, 11)
    first, second = jax.random.split(key)
    per_shard = NB // N_NEURON
    entries = KB * per_shard
    groups = N_SEGMENT * LMAX * N_NEURON
    keys = jax.random.split(first, groups)
    orders = jax.vmap(lambda single: jax.random.permutation(single, entries))(keys)
    source = orders % N_NEURON
    local = jax.random.randint(second, (groups, entries), 0, per_shard)
    first_row = jnp.arange(groups)[:, None] == 0
    local = jnp.where(first_row & (orders == 0), 0, local)
    local = jnp.where(first_row & (orders == N_NEURON - 1), per_shard - 1, local)
    index = source * per_shard + local
    index = index.reshape(N_SEGMENT, LMAX, N_NEURON, KB, per_shard)
    index = jnp.transpose(index, (0, 1, 3, 2, 4)).reshape(N_SEGMENT, LMAX, KB, NB)
    return index.astype(jnp.int32)


def shard_levels(own_key, extent, shards, low, largest):
    def one(position, shards_of):
        steps = jax.random.uniform(jax.random.fold_in(jax.random.fold_in(own_key, 6), position), (shards_of,), jnp.float32, low / len(shards), largest / len(shards))
        return jnp.repeat(jnp.exp(steps), extent[position] // shards_of).reshape((-1,) + (1,) * (len(extent) - position - 1))

    gain = one(*shards[0])
    for cut in shards[1:]:
        gain = gain * one(*cut)
    return gain


def gaussian(own_key, extent, scale, bound, shards=(), kind=jnp.bfloat16):
    gain = shard_levels(own_key, extent, shards, -0.22, 0.18) if shards else 1.0
    values = jax.random.normal(own_key, extent, jnp.float32) * scale * gain
    return jnp.minimum(jnp.maximum(values, -bound), bound).astype(kind)


def setup_inputs(seed: int = 0) -> dict:
    seeds = jax.random.split(jax.random.key(seed), 7)
    pending_minibatch = jnp.clip(32.0 * jax.random.uniform(seeds[0], (N_SEGMENT, SMALL_BATCH_SIZE, UNITS_OF_LEVEL), jnp.float32) ** shard_levels(seeds[0], (N_SEGMENT, SMALL_BATCH_SIZE, UNITS_OF_LEVEL), ((0, 32), (2, 16)), -0.2, 0.2), 0.0, 32.0).astype(jnp.bfloat16)
    arriving_minibatches = jnp.clip(32.0 * jax.random.uniform(seeds[1], (STEPS - 1, SMALL_BATCH_SIZE, UNITS_OF_LEVEL), jnp.float32) ** shard_levels(seeds[1], (STEPS - 1, SMALL_BATCH_SIZE, UNITS_OF_LEVEL), ((2, 16),), -0.2, 0.2), 0.0, 32.0).astype(jnp.bfloat16)
    coefficient_tiles = gaussian(seeds[2], (N_SEGMENT, LMAX, KB, BLK, UNITS_OF_LEVEL), (KB * BLK) ** -0.5, 0.375, ((0, 32), (4, 16)))
    offset_vector = jnp.clip(-4.0 + 6.0 * jax.random.uniform(seeds[3], (N_SEGMENT, LMAX, UNITS_OF_LEVEL), jnp.float32) ** shard_levels(seeds[3], (N_SEGMENT, LMAX, UNITS_OF_LEVEL), ((0, 32), (2, 16)), -0.2, 0.2), -4.0, 2.0)
    source_tile_lookup = draw_source_tile_lookup(jax.random.fold_in(seeds[6], 71), 0)
    depth_of_segment = draw_depth_of_segment(jax.random.fold_in(seeds[6], 71), 0)
    return {"pending_minibatch": pending_minibatch, "arriving_minibatches": arriving_minibatches, "coefficient_tiles": coefficient_tiles, "offset_vector": offset_vector, "source_tile_lookup": source_tile_lookup, "depth_of_segment": depth_of_segment}


def layer(y, w, b, idx):
    cols = idx[:, :, None] * BLK + jnp.arange(BLK, dtype=jnp.int32)[None, None, :]
    taken = jnp.take(y, cols.reshape(-1).astype(jnp.int32), axis=1)
    taken = taken.reshape(y.shape[0], KB, NB, BLK).astype(jnp.float32)
    wr = w.reshape(KB, BLK, NB, BLK).astype(jnp.float32)
    acc = jnp.einsum('bkjr,krjc->bjc', taken, wr).reshape(y.shape[0], UNITS_OF_LEVEL)
    return jnp.clip(acc + b[None, :], 0.0, 32.0).astype(jnp.bfloat16)


def segment_ordinal(args):
    y, w, b, idx, stored_tile_total = args
    for level in range(LMAX):
        fresh = layer(y, w[level], b[level], idx[level])
        y = jnp.where(level < stored_tile_total, fresh, y)
    return y


def reference(pending_minibatch, arriving_minibatches, coefficient_tiles, offset_vector, source_tile_lookup, depth_of_segment):
    activation_matrix = lax.map(segment_ordinal, (pending_minibatch, coefficient_tiles, offset_vector, source_tile_lookup, depth_of_segment))
    for step in range(1, STEPS):
        moved = jnp.concatenate([arriving_minibatches[step - 1][None], activation_matrix[:-1]], axis=0)
        activation_matrix = lax.map(segment_ordinal, (moved, coefficient_tiles, offset_vector, source_tile_lookup, depth_of_segment))
    return activation_matrix
```

```python
import functools

import jax
import jax.numpy as jnp
from jax import lax
from jax.experimental import pallas as pl
from jax.experimental.pallas import tpu as pltpu
from jax.sharding import PartitionSpec as P

BLK = 64
KB = 4
LMAX = 2
STAGES = 4
LANES = 128
SIDE = 4
MESH = pl.DeviceIdType.MESH


def torus_distance(step):
    return sum(min(c, SIDE - c) for c in step)


STEPS_FAR = sorted(
    ((dy, dx) for dy in range(SIDE) for dx in range(SIDE)), key=lambda s: -torus_distance(s)
)
STEPS_NEAR = sorted(
    ((dy, dx) for dy in range(SIDE) for dx in range(SIDE)), key=torus_distance
)


def lists_of_blocks(idx_ref, shards, per_source):
    rows = LMAX * KB
    per_shard = idx_ref.shape[-1]
    shard = lax.broadcasted_iota(jnp.int32, (shards, per_shard), 0)
    place = lax.broadcasted_iota(jnp.int32, (LANES, per_shard), 0)
    before = (
        lax.broadcasted_iota(jnp.int32, (per_shard, per_shard), 0)
        < lax.broadcasted_iota(jnp.int32, (per_shard, per_shard), 1)
    ).astype(jnp.bfloat16)
    entries = [idx_ref[0, r // KB, pl.ds(r % KB, 1), :] for r in range(rows)]
    sources = [e // per_shard for e in entries]
    masks = [(jnp.broadcast_to(s, shard.shape) == shard).astype(jnp.float32) for s in sources]
    ahead = jnp.dot(
        jnp.concatenate(masks, axis=0).astype(jnp.bfloat16),
        before,
        preferred_element_type=jnp.float32,
    )
    wanted = jnp.zeros((shards, LANES), jnp.float32)
    slots = []
    for level in range(LMAX):
        count = jnp.zeros((shards, 1), jnp.float32)
        for k in range(KB):
            r = level * KB + k
            mask = masks[r]
            rank = jnp.sum(
                mask * (ahead[r * shards : (r + 1) * shards] + count), axis=0, keepdims=True
            ).astype(jnp.int32)
            rank = jnp.clip(rank, 0, per_source - 1)
            side, pair = rank & 1, rank >> 1
            count = count + jnp.sum(mask, axis=1, keepdims=True)
            tile = sources[r] * (per_source // 2) + pair
            slots.append(tile + (side ^ (k & 1)) * (shards * per_source // 2))
            local = entries[r] & (per_shard - 1)
            local = ((local >> 1) + ((local ^ rank) & 1) * (per_shard // 2)).astype(jnp.float32)
            chosen = (mask * local).astype(jnp.bfloat16)
            placed = (
                jnp.broadcast_to(rank + level * per_source, place.shape) == place
            ).astype(jnp.bfloat16)
            wanted = wanted + lax.dot_general(
                chosen, placed, (((1,), (1,)), ((), ())), preferred_element_type=jnp.float32
            )
    return jnp.clip(wanted.astype(jnp.int32), 0, per_shard - 1), slots


def kernel(
    segments,
    shards,
    depth_ref,
    pending_ref,
    arriving_ref,
    weight_ref,
    offset_ref,
    idx_ref,
    out_ref,
    weights,
    own,
    send,
    recv,
    table,
    bias,
    entering,
    wants,
    arrived,
    slot_vmem,
    lists,
    slots,
    weight_sem,
    slot_sem,
    row_sem,
    list_send_sem,
    list_sem,
    next_send_sem,
    next_sem,
    send_sem,
    recv_sem,
):
    seg = lax.axis_index("segment")
    me = lax.axis_index("neuron")
    after = lax.rem(seg + 1, segments)
    ahead = lax.rem(seg + segments - 1, segments)
    row, col = lax.div(me, SIDE), lax.rem(me, SIDE)

    def peer(step):
        return lax.rem(row + step[0], SIDE) * SIDE + lax.rem(col + step[1], SIDE)

    far = [peer(s) for s in STEPS_FAR]
    near = [peer(s) for s in STEPS_NEAR]
    blocks = idx_ref.shape[-1]
    per_source = KB * blocks // shards
    tall = per_source * 4
    column_tiles = weights.shape[1]
    pairs = column_tiles
    low = lax.broadcasted_iota(jnp.int32, (8, LANES), 1) < BLK

    barrier = pltpu.get_barrier_semaphore()
    for p in far[:-1]:
        pl.semaphore_signal(barrier, inc=1, device_id=(seg, p), device_id_type=MESH)
    pl.semaphore_signal(barrier, inc=1, device_id=(after, me), device_id_type=MESH)
    pl.semaphore_signal(barrier, inc=1, device_id=(ahead, me), device_id_type=MESH)

    def weight_copy(level, c):
        return pltpu.make_async_copy(
            weight_ref.at[0, level, :, :, pl.ds(pl.multiple_of(c * LANES, LANES), LANES)],
            weights.at[level, c],
            weight_sem.at[level],
        )

    for level in range(LMAX):

        @pl.loop(0, column_tiles)
        def _(c):
            weight_copy(level, c).start()

    wanted, landing = lists_of_blocks(idx_ref, shards, per_source)
    for v in range(shards):
        wants[v] = wanted[v : v + 1]
    for r in range(LMAX * KB):
        slot_vmem[r, :, pl.ds(0, blocks)] = landing[r]
    slot_copy = pltpu.make_async_copy(slot_vmem, slots, slot_sem)
    slot_copy.start()

    def keep(tiles):
        tiles = tiles.reshape(pairs, 8, LANES)
        own[pl.ds(0, pairs)] = tiles
        own[pl.ds(pairs, pairs)] = pltpu.roll(tiles, BLK, 2)

    def tiles_of(ref):
        return jnp.concatenate(
            [ref[0, :, pl.ds(p * LANES, LANES)] for p in range(pairs)], axis=0
        ).astype(jnp.float32)

    for level in range(LMAX):
        for p in range(pairs):
            bias[level, p] = offset_ref[0, pl.ds(level, 1), pl.ds(p * LANES, LANES)]
    entering[...] = tiles_of(arriving_ref)
    keep(tiles_of(pending_ref))

    pl.semaphore_wait(barrier, len(far) + 1)

    def list_copy(p):
        return pltpu.make_async_remote_copy(
            src_ref=wants.at[p],
            dst_ref=arrived.at[me],
            send_sem=list_send_sem,
            recv_sem=list_sem.at[me],
            device_id=(seg, p),
            device_id_type=MESH,
        )

    for p in far[:-1]:
        list_copy(p).start()
    pltpu.make_async_copy(wants.at[me], arrived.at[me], list_sem.at[me]).start()

    def row_copy(p):
        return pltpu.make_async_copy(arrived.at[p], lists.at[p], row_sem.at[p])

    def list_take(p):
        pltpu.make_async_copy(wants.at[p], arrived.at[p], list_sem.at[p]).wait()
        row_copy(p).start()

    def gather_for(t, level, first_row, p):
        at = level * per_source
        row = first_row + p
        even, odd = (
            jnp.concatenate([own[lists[row, 0, at + 2 * q + h]] for q in range(per_source // 2)], axis=0)
            for h in range(2)
        )
        side = jnp.concatenate([low] * (per_source // 2), axis=0)
        send[t, block_rows(p), :] = jnp.where(side, even, odd).astype(jnp.bfloat16)

    def block_rows(p):
        return pl.ds(pl.multiple_of(p * tall, tall), tall)

    def data_copy(t, s, p):
        return pltpu.make_async_remote_copy(
            src_ref=send.at[t, block_rows(p)],
            dst_ref=recv.at[t, block_rows(me)],
            send_sem=send_sem.at[t],
            recv_sem=recv_sem.at[t],
            device_id=(s, p),
            device_id_type=MESH,
        )

    depth = depth_ref[0]

    def run(t):
        level = t % 2
        across = t == 2
        first_row = shards if across else 0
        s = after if across else seg
        order = near if t == 0 else far
        if across:
            later = pl.ds(shards, shards)
            pltpu.make_async_copy(wants, arrived.at[later], next_sem).wait()
            every = pltpu.make_async_copy(arrived.at[later], lists.at[later], slot_sem)
            every.start()
            every.wait()
        if t == 0:
            for p in order:
                list_take(p)
        for i, p in enumerate(order):
            local = STEPS_NEAR[i] == (0, 0) if t == 0 else STEPS_FAR[i] == (0, 0)
            if t == 0:
                row_copy(p).wait()
            gather_for(t, level, first_row, p)
            if local and not across:
                pltpu.make_async_copy(
                    send.at[t, block_rows(p)], recv.at[t, block_rows(p)], recv_sem.at[t]
                ).start()
            else:
                data_copy(t, s, p).start()
        if t == 0:
            for p in far:
                pltpu.make_async_remote_copy(
                    src_ref=wants.at[p],
                    dst_ref=arrived.at[shards + me],
                    send_sem=next_send_sem,
                    recv_sem=next_sem,
                    device_id=(ahead, p),
                    device_id_type=MESH,
                ).start()
            slot_copy.wait()
        if t < 2:
            pltpu.make_async_copy(
                weight_ref.at[0, level],
                weight_ref.at[0, level],
                weight_sem.at[level],
            ).wait()
        pltpu.make_async_copy(send.at[t], recv.at[t], recv_sem.at[t]).wait()
        half = shards * per_source // 2
        for v in range(shards):
            got = recv[t, pl.ds(v * tall, tall), :].astype(jnp.float32)
            got = got.reshape(per_source // 2, 8, LANES)
            table[pl.ds(v * (per_source // 2), per_source // 2)] = got
            table[pl.ds(half + v * (per_source // 2), per_source // 2)] = pltpu.roll(got, BLK, 2)
        side = jnp.concatenate([low] * 4, axis=0)
        fresh = []
        for c in range(column_tiles // 2):
            left = []
            for pair in range(KB // 2):
                a, b = (
                    jnp.concatenate(
                        [table[slots[level * KB + 2 * pair + h, 0, 4 * c + j]] for j in range(4)], axis=0
                    )
                    for h in range(2)
                )
                left.append(jnp.where(side, a, b))
            left = jnp.concatenate(left, axis=1).astype(jnp.bfloat16)
            right = jnp.concatenate(
                [weights[level, 2 * c + i].reshape(KB * BLK, LANES) for i in range(2)], axis=1
            )
            total = jnp.dot(left, right, preferred_element_type=jnp.float32)
            fresh.append(jnp.where(low, total[0:8, 0:LANES], total[8:16, 0:LANES]))
            fresh.append(jnp.where(low, total[16:24, LANES:], total[24:32, LANES:]))
        fresh = jnp.concatenate(fresh, axis=0).reshape(pairs, 8, LANES) + bias[level]
        fresh = jnp.clip(fresh, 0.0, 32.0).astype(jnp.bfloat16).astype(jnp.float32)
        if level > 0:
            fresh = jnp.where(depth > level, fresh, own[pl.ds(0, pairs)])
        if t == 1:
            fresh = jnp.where(seg == segments - 1, entering[...].reshape(fresh.shape), fresh)
        if t < STAGES - 1:
            keep(fresh)
        else:
            for p in range(pairs):
                out_ref[0, :, pl.ds(p * LANES, LANES)] = fresh[p].astype(jnp.bfloat16)

    for t in range(STAGES):
        run(t)

    some = pl.ds(0, (shards - 1) * tall)
    for t in range(STAGES):
        rows = pl.ds(0, shards * tall) if t == 2 else some
        pltpu.make_async_copy(send.at[t, rows], recv.at[t, rows], send_sem.at[t]).wait()
    pltpu.make_async_copy(
        wants.at[pl.ds(0, shards - 1)], arrived.at[pl.ds(0, shards - 1)], list_send_sem
    ).wait()
    pltpu.make_async_copy(wants, arrived.at[pl.ds(0, shards)], next_send_sem).wait()


def solution(mesh):
    segments, shards = mesh.shape["segment"], mesh.shape["neuron"]

    def per_device(pending, arriving, coefficients, offsets, lookup, depth):
        rows, wide = pending.shape[1:]
        blocks = lookup.shape[-1]
        per_source = KB * blocks // shards
        tall = per_source * 4
        vmem = pl.BlockSpec(memory_space=pltpu.VMEM)
        return pl.pallas_call(
            functools.partial(kernel, segments, shards),
            out_shape=jax.ShapeDtypeStruct(pending.shape, jnp.bfloat16),
            in_specs=[
                pl.BlockSpec(memory_space=pltpu.SMEM),
                vmem,
                vmem,
                pl.BlockSpec(memory_space=pl.ANY),
                vmem,
                vmem,
            ],
            out_specs=vmem,
            scratch_shapes=[
                pltpu.VMEM((LMAX, wide // LANES, KB, BLK, LANES), jnp.bfloat16),
                pltpu.VMEM((blocks, rows, LANES), jnp.float32),
                pltpu.VMEM((STAGES, shards * tall, LANES), jnp.bfloat16),
                pltpu.VMEM((STAGES, shards * tall, LANES), jnp.bfloat16),
                pltpu.VMEM((shards * per_source, rows, LANES), jnp.float32),
                pltpu.VMEM((LMAX, wide // LANES, 1, LANES), jnp.float32),
                pltpu.VMEM((wide // LANES * rows, LANES), jnp.float32),
                pltpu.VMEM((shards, 1, LANES), jnp.int32),
                pltpu.VMEM((2 * shards, 1, LANES), jnp.int32),
                pltpu.VMEM((LMAX * KB, 1, LANES), jnp.int32),
                pltpu.SMEM((2 * shards, 1, LANES), jnp.int32),
                pltpu.SMEM((LMAX * KB, 1, LANES), jnp.int32),
                pltpu.SemaphoreType.DMA((LMAX,)),
                pltpu.SemaphoreType.DMA,
                pltpu.SemaphoreType.DMA((shards,)),
                pltpu.SemaphoreType.DMA,
                pltpu.SemaphoreType.DMA((shards,)),
                pltpu.SemaphoreType.DMA,
                pltpu.SemaphoreType.DMA,
                pltpu.SemaphoreType.DMA((STAGES,)),
                pltpu.SemaphoreType.DMA((STAGES,)),
            ],
            compiler_params=pltpu.CompilerParams(
                collective_id=0, has_side_effects=True, vmem_limit_bytes=32 * 1024 * 1024
            ),
        )(depth, pending, arriving, coefficients, offsets, lookup)

    placed = (
        P("segment", None, "neuron"),
        P(None, None, "neuron"),
        P("segment", None, None, None, "neuron"),
        P("segment", None, "neuron"),
        P("segment", None, None, "neuron"),
        P("segment"),
    )
    return jax.shard_map(
        per_device,
        mesh=mesh,
        in_specs=placed,
        out_specs=P("segment", None, "neuron"),
        check_vma=False,
    )
```

```python
import functools

import jax
import jax.numpy as jnp
from jax import lax
from jax.experimental import pallas as pl
from jax.experimental.pallas import tpu as pltpu
from jax.sharding import PartitionSpec as P

BLK = 64
KB = 4
LMAX = 2
STAGES = 4
NEAR = 11
LANES = 128
SIDE = 4
MESH = pl.DeviceIdType.MESH


def torus_distance(step):
    return sum(min(c, SIDE - c) for c in step)


STEPS_FAR = sorted(
    ((dy, dx) for dy in range(SIDE) for dx in range(SIDE)), key=lambda s: -torus_distance(s)
)
STEPS_NEAR = sorted(
    ((dy, dx) for dy in range(SIDE) for dx in range(SIDE)), key=torus_distance
)


def lists_of_blocks(idx_ref, shards, per_source):
    rows = LMAX * KB
    per_shard = idx_ref.shape[-1]
    shard = lax.broadcasted_iota(jnp.int32, (shards, per_shard), 0)
    place = lax.broadcasted_iota(jnp.int32, (LANES, per_shard), 0)
    before = (
        lax.broadcasted_iota(jnp.int32, (per_shard, per_shard), 0)
        < lax.broadcasted_iota(jnp.int32, (per_shard, per_shard), 1)
    ).astype(jnp.bfloat16)
    entries = [idx_ref[0, r // KB, pl.ds(r % KB, 1), :] for r in range(rows)]
    sources = [e // per_shard for e in entries]
    masks = [(jnp.broadcast_to(s, shard.shape) == shard).astype(jnp.float32) for s in sources]
    ahead = jnp.dot(
        jnp.concatenate(masks, axis=0).astype(jnp.bfloat16),
        before,
        preferred_element_type=jnp.float32,
    )
    wanted = jnp.zeros((shards, LANES), jnp.float32)
    slots = []
    for level in range(LMAX):
        count = jnp.zeros((shards, 1), jnp.float32)
        for k in range(KB):
            r = level * KB + k
            mask = masks[r]
            rank = jnp.sum(
                mask * (ahead[r * shards : (r + 1) * shards] + count), axis=0, keepdims=True
            ).astype(jnp.int32)
            rank = jnp.clip(rank, 0, per_source - 1)
            side, pair = rank & 1, rank >> 1
            count = count + jnp.sum(mask, axis=1, keepdims=True)
            tile = sources[r] * (per_source // 2) + pair
            slots.append(tile + (side ^ (k & 1)) * (shards * per_source // 2))
            local = entries[r] & (per_shard - 1)
            local = ((local >> 1) + ((local ^ rank) & 1) * (per_shard // 2)).astype(jnp.float32)
            chosen = (mask * local).astype(jnp.bfloat16)
            placed = (
                jnp.broadcast_to(rank + level * per_source, place.shape) == place
            ).astype(jnp.bfloat16)
            wanted = wanted + lax.dot_general(
                chosen, placed, (((1,), (1,)), ((), ())), preferred_element_type=jnp.float32
            )
    return jnp.clip(wanted.astype(jnp.int32), 0, per_shard - 1), slots


def kernel(
    segments,
    shards,
    depth_ref,
    pending_ref,
    arriving_ref,
    weight_ref,
    offset_ref,
    idx_ref,
    out_ref,
    pending,
    arriving,
    offsets,
    idx,
    weights,
    own,
    entering,
    send,
    send_entering,
    recv,
    table,
    bias,
    wants,
    arrived,
    slot_vmem,
    lists,
    slots,
    load_sem,
    weight_sem,
    slot_sem,
    row_sem,
    list_send_sem,
    list_sem,
    next_send_sem,
    next_sem,
    next_here,
    send_sem,
    send_entering_sem,
    recv_sem,
):
    seg = lax.axis_index("segment")
    me = lax.axis_index("neuron")
    first, last = seg == 0, seg == segments - 1
    after = lax.rem(seg + 1, segments)
    ahead = lax.rem(seg + segments - 1, segments)
    row, col = lax.div(me, SIDE), lax.rem(me, SIDE)

    def peer(step):
        return lax.rem(row + step[0], SIDE) * SIDE + lax.rem(col + step[1], SIDE)

    far = [peer(s) for s in STEPS_FAR]
    near = [peer(s) for s in STEPS_NEAR]
    blocks = idx_ref.shape[-1]
    per_source = KB * blocks // shards
    tall = per_source * 4
    column_tiles = weights.shape[-1] // LANES
    pairs = column_tiles
    low = lax.broadcasted_iota(jnp.int32, (8, LANES), 1) < BLK

    load = [
        pltpu.make_async_copy(source, target, load_sem.at[i])
        for i, (source, target) in enumerate(
            ((idx_ref, idx), (pending_ref, pending), (offset_ref, offsets), (arriving_ref, arriving))
        )
    ]
    load[0].start()
    barrier = pltpu.get_barrier_semaphore()
    for p in far[:-1]:
        pl.semaphore_signal(barrier, inc=1, device_id=(seg, p), device_id_type=MESH)

    @pl.when(jnp.logical_not(last))
    def _():
        pl.semaphore_signal(barrier, inc=1, device_id=(after, me), device_id_type=MESH)

    for copy in load[1:]:
        copy.start()

    load[0].wait()
    wanted, landing = lists_of_blocks(idx, shards, per_source)
    for v in range(shards):
        wants[v] = wanted[v : v + 1]

    pl.semaphore_wait(barrier, jnp.where(first, shards - 1, shards))

    def list_copy(p):
        return pltpu.make_async_remote_copy(
            src_ref=wants.at[p],
            dst_ref=arrived.at[me],
            send_sem=list_send_sem,
            recv_sem=list_sem.at[me],
            device_id=(seg, p),
            device_id_type=MESH,
        )

    for p in far[:-1]:
        list_copy(p).start()
    pltpu.make_async_copy(wants.at[me], arrived.at[me], list_sem.at[me]).start()

    @pl.when(jnp.logical_not(first))
    def _():
        pl.semaphore_signal(next_here, inc=1, device_id=(ahead, me), device_id_type=MESH)

    for r in range(LMAX * KB):
        slot_vmem[r, :, pl.ds(0, blocks)] = landing[r]
    slot_copy = pltpu.make_async_copy(slot_vmem, slots, slot_sem)
    slot_copy.start()

    for level in range(LMAX):
        pltpu.make_async_copy(
            weight_ref.at[0, level], weights.at[level], weight_sem.at[level]
        ).start()

    def keep(tiles, where):
        tiles = tiles.reshape(pairs, 8, LANES)
        where[pl.ds(0, pairs)] = tiles
        where[pl.ds(pairs, pairs)] = pltpu.roll(tiles, BLK, 2)

    def tiles_of(ref):
        return jnp.concatenate(
            [ref[0, :, pl.ds(p * LANES, LANES)] for p in range(pairs)], axis=0
        ).astype(jnp.float32)

    load[1].wait()
    keep(tiles_of(pending), own)
    load[2].wait()
    for level in range(LMAX):
        for p in range(pairs):
            bias[level, p] = offsets[0, pl.ds(level, 1), pl.ds(p * LANES, LANES)]

    def row_copy(p):
        return pltpu.make_async_copy(arrived.at[p], lists.at[p], row_sem.at[p])

    def list_take(p):
        pltpu.make_async_copy(wants.at[p], arrived.at[p], list_sem.at[p]).wait()
        row_copy(p).start()

    def gather_for(where, level, row, target, p):
        at = level * per_source
        even, odd = (
            jnp.concatenate(
                [where[lists[row, 0, at + 2 * q + h]] for q in range(per_source // 2)], axis=0
            )
            for h in range(2)
        )
        side = jnp.concatenate([low] * (per_source // 2), axis=0)
        target[block_rows(p), :] = jnp.where(side, even, odd).astype(jnp.bfloat16)

    def block_rows(p):
        return pl.ds(pl.multiple_of(p * tall, tall), tall)

    def give(t, s, p, source, sem, local):
        if local:
            pltpu.make_async_copy(
                source.at[block_rows(p)], recv.at[t, block_rows(p)], recv_sem.at[t, me]
            ).start()
            return
        pltpu.make_async_remote_copy(
            src_ref=source.at[block_rows(p)],
            dst_ref=recv.at[t, block_rows(me)],
            send_sem=sem,
            recv_sem=recv_sem.at[t, me],
            device_id=(s, p),
            device_id_type=MESH,
        ).start()

    depth = depth_ref[0]

    def send_first():
        def one(i):
            row_copy(near[i]).wait()
            gather_for(own, 0, near[i], send.at[0], near[i])
            give(0, seg, near[i], send.at[0], send_sem.at[0], i == 0)

        for group in (range(NEAR), range(NEAR, shards)):
            for i in group:
                list_take(near[i])
            for i in reversed(group):
                one(i)

        @pl.when(jnp.logical_not(first))
        def _():
            for p in far:
                pltpu.make_async_remote_copy(
                    src_ref=wants.at[p],
                    dst_ref=arrived.at[shards + me],
                    send_sem=next_send_sem,
                    recv_sem=next_sem,
                    device_id=(ahead, p),
                    device_id_type=MESH,
                ).start()

        load[3].wait()

        @pl.when(first)
        def _():
            keep(tiles_of(arriving), entering)
            for i, p in enumerate(far):
                gather_for(entering, 0, p, send_entering, p)
                give(2, seg, p, send_entering, send_entering_sem, i == shards - 1)

        slot_copy.wait()

    def send_within(t):
        for i, p in enumerate(far):
            gather_for(own, t % LMAX, p, send.at[t], p)
            give(t, seg, p, send.at[t], send_sem.at[t], i == shards - 1)

    def send_across(t):
        @pl.when(jnp.logical_not(last))
        def _():
            later = pl.ds(shards, shards)
            pltpu.make_async_copy(wants, arrived.at[later], next_sem).wait()
            every = pltpu.make_async_copy(arrived.at[later], lists.at[later], slot_sem)
            every.start()
            pl.semaphore_wait(next_here, 1)
            every.wait()
            for p in far:
                gather_for(own, 0, shards + p, send.at[t], p)
                give(t, after, p, send.at[t], send_sem.at[t], False)

    def apply(t):
        level = t % LMAX
        if t < LMAX:
            pltpu.make_async_copy(
                weight_ref.at[0, level], weight_ref.at[0, level], weight_sem.at[level]
            ).wait()
        half = shards * per_source // 2
        deep = per_source // 2
        for group in (near[:NEAR], near[NEAR:]):
            for v in group:
                pltpu.make_async_copy(
                    send.at[t, block_rows(v)], recv.at[t, block_rows(v)], recv_sem.at[t, v]
                ).wait()
            for v in group:
                got = recv[t, block_rows(v), :].astype(jnp.float32).reshape(deep, 8, LANES)
                table[pl.ds(v * deep, deep)] = got
                table[pl.ds(half + v * deep, deep)] = pltpu.roll(got, BLK, 2)
        side = jnp.concatenate([low] * 4, axis=0)
        fresh = []
        for c in range(column_tiles // 2):
            left = []
            for pair in range(KB // 2):
                a, b = (
                    jnp.concatenate(
                        [table[slots[level * KB + 2 * pair + h, 0, 4 * c + j]] for j in range(4)], axis=0
                    )
                    for h in range(2)
                )
                left.append(jnp.where(side, a, b))
            left = jnp.concatenate(left, axis=1).astype(jnp.bfloat16)
            right = weights[level, :, :, pl.ds(2 * c * LANES, 2 * LANES)]
            right = right.reshape(KB * BLK, 2 * LANES)
            total = jnp.dot(left, right, preferred_element_type=jnp.float32)
            fresh.append(jnp.where(low, total[0:8, 0:LANES], total[8:16, 0:LANES]))
            fresh.append(jnp.where(low, total[16:24, LANES:], total[24:32, LANES:]))
        fresh = jnp.concatenate(fresh, axis=0).reshape(pairs, 8, LANES) + bias[level]
        fresh = jnp.clip(fresh, 0.0, 32.0).astype(jnp.bfloat16).astype(jnp.float32)
        if level > 0:
            fresh = jnp.where(depth > level, fresh, own[pl.ds(0, pairs)])
        if t < STAGES - 1:
            keep(fresh, own)
        else:
            for p in range(pairs):
                out_ref[0, :, pl.ds(p * LANES, LANES)] = fresh[p].astype(jnp.bfloat16)

    send_first()
    apply(0)
    send_within(1)
    apply(1)
    send_across(2)
    apply(2)
    send_within(3)
    apply(3)

    def settle(rows, sem):
        pltpu.make_async_copy(send.at[0, rows], recv.at[0, rows], sem).wait()

    some, whole = pl.ds(0, (shards - 1) * tall), pl.ds(0, shards * tall)
    for t in (0, 1, 3):
        settle(some, send_sem.at[t])

    @pl.when(jnp.logical_not(last))
    def _():
        settle(whole, send_sem.at[2])

    @pl.when(first)
    def _():
        settle(some, send_entering_sem)

    pltpu.make_async_copy(
        wants.at[pl.ds(0, shards - 1)], arrived.at[pl.ds(0, shards - 1)], list_send_sem
    ).wait()

    @pl.when(jnp.logical_not(first))
    def _():
        pltpu.make_async_copy(wants, arrived.at[pl.ds(0, shards)], next_send_sem).wait()


def solution(mesh):
    segments, shards = mesh.shape["segment"], mesh.shape["neuron"]

    def per_device(pending, arriving, coefficients, offsets, lookup, depth):
        rows, wide = pending.shape[1:]
        blocks = lookup.shape[-1]
        per_source = KB * blocks // shards
        tall = per_source * 4
        pairs = wide // LANES
        anywhere = pl.BlockSpec(memory_space=pl.ANY)
        return pl.pallas_call(
            functools.partial(kernel, segments, shards),
            out_shape=jax.ShapeDtypeStruct(pending.shape, jnp.bfloat16),
            in_specs=[pl.BlockSpec(memory_space=pltpu.SMEM)] + [anywhere] * 5,
            out_specs=pl.BlockSpec(memory_space=pltpu.VMEM),
            scratch_shapes=[
                pltpu.VMEM(pending.shape, jnp.bfloat16),
                pltpu.VMEM(arriving.shape, jnp.bfloat16),
                pltpu.VMEM(offsets.shape, jnp.float32),
                pltpu.VMEM(lookup.shape, jnp.int32),
                pltpu.VMEM((LMAX, KB, BLK, wide), jnp.bfloat16),
                pltpu.VMEM((blocks, rows, LANES), jnp.float32),
                pltpu.VMEM((blocks, rows, LANES), jnp.float32),
                pltpu.VMEM((STAGES, shards * tall, LANES), jnp.bfloat16),
                pltpu.VMEM((shards * tall, LANES), jnp.bfloat16),
                pltpu.VMEM((STAGES, shards * tall, LANES), jnp.bfloat16),
                pltpu.VMEM((shards * per_source, rows, LANES), jnp.float32),
                pltpu.VMEM((LMAX, pairs, 1, LANES), jnp.float32),
                pltpu.VMEM((shards, 1, LANES), jnp.int32),
                pltpu.VMEM((2 * shards, 1, LANES), jnp.int32),
                pltpu.VMEM((LMAX * KB, 1, LANES), jnp.int32),
                pltpu.SMEM((2 * shards, 1, LANES), jnp.int32),
                pltpu.SMEM((LMAX * KB, 1, LANES), jnp.int32),
                pltpu.SemaphoreType.DMA((4,)),
                pltpu.SemaphoreType.DMA((LMAX,)),
                pltpu.SemaphoreType.DMA,
                pltpu.SemaphoreType.DMA((shards,)),
                pltpu.SemaphoreType.DMA,
                pltpu.SemaphoreType.DMA((shards,)),
                pltpu.SemaphoreType.DMA,
                pltpu.SemaphoreType.DMA,
                pltpu.SemaphoreType.REGULAR,
                pltpu.SemaphoreType.DMA((STAGES,)),
                pltpu.SemaphoreType.DMA,
                pltpu.SemaphoreType.DMA((STAGES, shards)),
            ],
            compiler_params=pltpu.CompilerParams(
                collective_id=0, has_side_effects=True, vmem_limit_bytes=60 * 1024 * 1024
            ),
        )(depth, pending, arriving, coefficients, offsets, lookup)

    placed = (
        P("segment", None, "neuron"),
        P(None, None, "neuron"),
        P("segment", None, None, None, "neuron"),
        P("segment", None, "neuron"),
        P("segment", None, None, "neuron"),
        P("segment"),
    )
    return jax.shard_map(
        per_device,
        mesh=mesh,
        in_specs=placed,
        out_specs=P("segment", None, "neuron"),
        check_vma=False,
    )
```

```python
import functools

import jax
import jax.numpy as jnp
from jax import lax
from jax.experimental import pallas as pl
from jax.experimental.pallas import tpu as pltpu
from jax.sharding import PartitionSpec as P

BLK = 64
KB = 4
LMAX = 2
STAGES = 4
NEAR = 11
LANES = 128
SIDE = 4
MESH = pl.DeviceIdType.MESH


def torus_distance(step):
    return sum(min(c, SIDE - c) for c in step)


STEPS_FAR = sorted(
    ((dy, dx) for dy in range(SIDE) for dx in range(SIDE)), key=lambda s: -torus_distance(s)
)
STEPS_NEAR = sorted(
    ((dy, dx) for dy in range(SIDE) for dx in range(SIDE)), key=torus_distance
)


def lists_of_blocks(idx_ref, shards, per_source):
    rows = LMAX * KB
    per_shard = idx_ref.shape[-1]
    shard = lax.broadcasted_iota(jnp.int32, (shards, per_shard), 0)
    place = lax.broadcasted_iota(jnp.int32, (LANES, per_shard), 0)
    before = (
        lax.broadcasted_iota(jnp.int32, (per_shard, per_shard), 0)
        < lax.broadcasted_iota(jnp.int32, (per_shard, per_shard), 1)
    ).astype(jnp.bfloat16)
    entries = [idx_ref[0, r // KB, pl.ds(r % KB, 1), :] for r in range(rows)]
    sources = [e // per_shard for e in entries]
    masks = [(jnp.broadcast_to(s, shard.shape) == shard).astype(jnp.float32) for s in sources]
    ahead = jnp.dot(
        jnp.concatenate(masks, axis=0).astype(jnp.bfloat16),
        before,
        preferred_element_type=jnp.float32,
    )
    wanted = jnp.zeros((shards, LANES), jnp.float32)
    slots = []
    for level in range(LMAX):
        count = jnp.zeros((shards, 1), jnp.float32)
        for k in range(KB):
            r = level * KB + k
            mask = masks[r]
            rank = jnp.sum(
                mask * (ahead[r * shards : (r + 1) * shards] + count), axis=0, keepdims=True
            ).astype(jnp.int32)
            rank = jnp.clip(rank, 0, per_source - 1)
            side, pair = rank & 1, rank >> 1
            count = count + jnp.sum(mask, axis=1, keepdims=True)
            tile = sources[r] * (per_source // 2) + pair
            slots.append(tile + (side ^ (k & 1)) * (shards * per_source // 2))
            local = entries[r] & (per_shard - 1)
            local = ((local >> 1) + ((local ^ rank) & 1) * (per_shard // 2)).astype(jnp.float32)
            chosen = (mask * local).astype(jnp.bfloat16)
            placed = (
                jnp.broadcast_to(rank + level * per_source, place.shape) == place
            ).astype(jnp.bfloat16)
            wanted = wanted + lax.dot_general(
                chosen, placed, (((1,), (1,)), ((), ())), preferred_element_type=jnp.float32
            )
    return jnp.clip(wanted.astype(jnp.int32), 0, per_shard - 1), slots


def kernel(
    segments,
    shards,
    depth_ref,
    pending_ref,
    arriving_ref,
    weight_ref,
    offset_ref,
    idx_ref,
    out_ref,
    pending,
    arriving,
    offsets,
    idx,
    weights,
    own,
    entering,
    send,
    send_entering,
    recv,
    table,
    bias,
    wants,
    arrived,
    slot_vmem,
    lists,
    slots,
    load_sem,
    weight_sem,
    slot_sem,
    row_sem,
    list_send_sem,
    list_sem,
    next_send_sem,
    next_sem,
    next_here,
    send_sem,
    send_entering_sem,
    recv_sem,
):
    seg = lax.axis_index("segment")
    me = lax.axis_index("neuron")
    first, last = seg == 0, seg == segments - 1
    after = lax.rem(seg + 1, segments)
    ahead = lax.rem(seg + segments - 1, segments)
    row, col = lax.div(me, SIDE), lax.rem(me, SIDE)

    def peer(step):
        return lax.rem(row + step[0], SIDE) * SIDE + lax.rem(col + step[1], SIDE)

    far = [peer(s) for s in STEPS_FAR]
    near = [peer(s) for s in STEPS_NEAR]
    blocks = idx_ref.shape[-1]
    per_source = KB * blocks // shards
    tall = per_source * 4
    column_tiles = weights.shape[-1] // LANES
    pairs = column_tiles
    low = lax.broadcasted_iota(jnp.int32, (8, LANES), 1) < BLK

    load = [
        pltpu.make_async_copy(source, target, load_sem.at[i])
        for i, (source, target) in enumerate(
            ((idx_ref, idx), (pending_ref, pending), (offset_ref, offsets), (arriving_ref, arriving))
        )
    ]
    load[0].start()
    barrier = pltpu.get_barrier_semaphore()
    for p in far[:-1]:
        pl.semaphore_signal(barrier, inc=1, device_id=(seg, p), device_id_type=MESH)

    @pl.when(jnp.logical_not(last))
    def _():
        pl.semaphore_signal(barrier, inc=1, device_id=(after, me), device_id_type=MESH)

    for copy in load[1:]:
        copy.start()

    load[0].wait()
    wanted, landing = lists_of_blocks(idx, shards, per_source)
    for v in range(shards):
        wants[v] = wanted[v : v + 1]

    pl.semaphore_wait(barrier, jnp.where(first, shards - 1, shards))

    def list_copy(p):
        return pltpu.make_async_remote_copy(
            src_ref=wants.at[p],
            dst_ref=arrived.at[me],
            send_sem=list_send_sem,
            recv_sem=list_sem.at[me],
            device_id=(seg, p),
            device_id_type=MESH,
        )

    for p in far[:-1]:
        list_copy(p).start()
    pltpu.make_async_copy(wants.at[me], arrived.at[me], list_sem.at[me]).start()

    @pl.when(jnp.logical_not(first))
    def _():
        pl.semaphore_signal(next_here, inc=1, device_id=(ahead, me), device_id_type=MESH)

    for r in range(LMAX * KB):
        slot_vmem[r, :, pl.ds(0, blocks)] = landing[r]
    slot_copy = pltpu.make_async_copy(slot_vmem, slots, slot_sem)
    slot_copy.start()

    for level in range(LMAX):
        pltpu.make_async_copy(
            weight_ref.at[0, level], weights.at[level], weight_sem.at[level]
        ).start()

    def keep(tiles, where):
        tiles = tiles.reshape(pairs, 8, LANES)
        where[pl.ds(0, pairs)] = tiles
        where[pl.ds(pairs, pairs)] = pltpu.roll(tiles, BLK, 2)

    def tiles_of(ref):
        return jnp.concatenate(
            [ref[0, :, pl.ds(p * LANES, LANES)] for p in range(pairs)], axis=0
        ).astype(jnp.float32)

    load[1].wait()
    keep(tiles_of(pending), own)
    load[2].wait()
    for level in range(LMAX):
        for p in range(pairs):
            bias[level, p] = offsets[0, pl.ds(level, 1), pl.ds(p * LANES, LANES)]

    def row_copy(p):
        return pltpu.make_async_copy(arrived.at[p], lists.at[p], row_sem.at[p])

    def list_take(p):
        pltpu.make_async_copy(wants.at[p], arrived.at[p], list_sem.at[p]).wait()
        row_copy(p).start()

    def gather_for(where, level, row, target, p):
        at = level * per_source
        even, odd = (
            jnp.concatenate(
                [where[lists[row, 0, at + 2 * q + h]] for q in range(per_source // 2)], axis=0
            )
            for h in range(2)
        )
        side = jnp.concatenate([low] * (per_source // 2), axis=0)
        target[block_rows(p), :] = jnp.where(side, even, odd).astype(jnp.bfloat16)

    def block_rows(p):
        return pl.ds(pl.multiple_of(p * tall, tall), tall)

    def give(t, s, p, source, sem, local):
        if local:
            pltpu.make_async_copy(
                source.at[block_rows(p)], recv.at[t, block_rows(p)], recv_sem.at[t, me]
            ).start()
            return
        pltpu.make_async_remote_copy(
            src_ref=source.at[block_rows(p)],
            dst_ref=recv.at[t, block_rows(me)],
            send_sem=sem,
            recv_sem=recv_sem.at[t, me],
            device_id=(s, p),
            device_id_type=MESH,
        ).start()

    depth = depth_ref[0]

    def send_first():
        def one(i):
            row_copy(near[i]).wait()
            gather_for(own, 0, near[i], send.at[0], near[i])
            give(0, seg, near[i], send.at[0], send_sem.at[0], i == 0)

        for group in (range(NEAR), range(NEAR, shards)):
            for i in group:
                list_take(near[i])
            for i in reversed(group):
                one(i)

        @pl.when(jnp.logical_not(first))
        def _():
            for p in far:
                pltpu.make_async_remote_copy(
                    src_ref=wants.at[p],
                    dst_ref=arrived.at[shards + me],
                    send_sem=next_send_sem,
                    recv_sem=next_sem,
                    device_id=(ahead, p),
                    device_id_type=MESH,
                ).start()

        load[3].wait()

        @pl.when(first)
        def _():
            keep(tiles_of(arriving), entering)
            for i, p in enumerate(far):
                gather_for(entering, 0, p, send_entering, p)
                give(2, seg, p, send_entering, send_entering_sem, i == shards - 1)

        slot_copy.wait()

    def send_within(t):
        for i, p in enumerate(far):
            gather_for(own, t % LMAX, p, send.at[t], p)
            give(t, seg, p, send.at[t], send_sem.at[t], i == shards - 1)

    def take_next_lists():
        later = pl.ds(shards, shards)

        @pl.when(jnp.logical_not(last))
        def _():
            pltpu.make_async_copy(wants, arrived.at[later], next_sem).wait()
            every = pltpu.make_async_copy(arrived.at[later], lists.at[later], slot_sem)
            every.start()
            pl.semaphore_wait(next_here, 1)
            every.wait()

    def send_across(t):
        @pl.when(jnp.logical_not(last))
        def _():
            for p in far:
                gather_for(own, 0, shards + p, send.at[t], p)
                give(t, after, p, send.at[t], send_sem.at[t], False)

    def apply(t):
        level = t % LMAX
        if t < LMAX:
            pltpu.make_async_copy(
                weight_ref.at[0, level], weight_ref.at[0, level], weight_sem.at[level]
            ).wait()
        half = shards * per_source // 2
        deep = per_source // 2
        for group in (near[:NEAR], near[NEAR:]):
            for v in group:
                pltpu.make_async_copy(
                    send.at[t, block_rows(v)], recv.at[t, block_rows(v)], recv_sem.at[t, v]
                ).wait()
            for v in group:
                got = recv[t, block_rows(v), :].astype(jnp.float32).reshape(deep, 8, LANES)
                table[pl.ds(v * deep, deep)] = got
                table[pl.ds(half + v * deep, deep)] = pltpu.roll(got, BLK, 2)
        side = jnp.concatenate([low] * 4, axis=0)
        fresh = []
        for c in range(column_tiles // 2):
            left = []
            for pair in range(KB // 2):
                a, b = (
                    jnp.concatenate(
                        [table[slots[level * KB + 2 * pair + h, 0, 4 * c + j]] for j in range(4)], axis=0
                    )
                    for h in range(2)
                )
                left.append(jnp.where(side, a, b))
            left = jnp.concatenate(left, axis=1).astype(jnp.bfloat16)
            right = weights[level, :, :, pl.ds(2 * c * LANES, 2 * LANES)]
            right = right.reshape(KB * BLK, 2 * LANES)
            total = jnp.dot(left, right, preferred_element_type=jnp.float32)
            fresh.append(jnp.where(low, total[0:8, 0:LANES], total[8:16, 0:LANES]))
            fresh.append(jnp.where(low, total[16:24, LANES:], total[24:32, LANES:]))
        fresh = jnp.concatenate(fresh, axis=0).reshape(pairs, 8, LANES) + bias[level]
        fresh = jnp.clip(fresh, 0.0, 32.0).astype(jnp.bfloat16).astype(jnp.float32)
        if level > 0:
            fresh = jnp.where(depth > level, fresh, own[pl.ds(0, pairs)])
        if t < STAGES - 1:
            keep(fresh, own)
        else:
            for p in range(pairs):
                out_ref[0, :, pl.ds(p * LANES, LANES)] = fresh[p].astype(jnp.bfloat16)

    send_first()
    apply(0)
    send_within(1)
    take_next_lists()
    apply(1)
    send_across(2)
    apply(2)
    send_within(3)
    apply(3)

    def settle(rows, sem):
        pltpu.make_async_copy(send.at[0, rows], recv.at[0, rows], sem).wait()

    some, whole = pl.ds(0, (shards - 1) * tall), pl.ds(0, shards * tall)
    for t in (0, 1, 3):
        settle(some, send_sem.at[t])

    @pl.when(jnp.logical_not(last))
    def _():
        settle(whole, send_sem.at[2])

    @pl.when(first)
    def _():
        settle(some, send_entering_sem)

    pltpu.make_async_copy(
        wants.at[pl.ds(0, shards - 1)], arrived.at[pl.ds(0, shards - 1)], list_send_sem
    ).wait()

    @pl.when(jnp.logical_not(first))
    def _():
        pltpu.make_async_copy(wants, arrived.at[pl.ds(0, shards)], next_send_sem).wait()


def solution(mesh):
    segments, shards = mesh.shape["segment"], mesh.shape["neuron"]

    def per_device(pending, arriving, coefficients, offsets, lookup, depth):
        rows, wide = pending.shape[1:]
        blocks = lookup.shape[-1]
        per_source = KB * blocks // shards
        tall = per_source * 4
        pairs = wide // LANES
        anywhere = pl.BlockSpec(memory_space=pl.ANY)
        return pl.pallas_call(
            functools.partial(kernel, segments, shards),
            out_shape=jax.ShapeDtypeStruct(pending.shape, jnp.bfloat16),
            in_specs=[pl.BlockSpec(memory_space=pltpu.SMEM)] + [anywhere] * 5,
            out_specs=pl.BlockSpec(memory_space=pltpu.VMEM),
            scratch_shapes=[
                pltpu.VMEM(pending.shape, jnp.bfloat16),
                pltpu.VMEM(arriving.shape, jnp.bfloat16),
                pltpu.VMEM(offsets.shape, jnp.float32),
                pltpu.VMEM(lookup.shape, jnp.int32),
                pltpu.VMEM((LMAX, KB, BLK, wide), jnp.bfloat16),
                pltpu.VMEM((blocks, rows, LANES), jnp.float32),
                pltpu.VMEM((blocks, rows, LANES), jnp.float32),
                pltpu.VMEM((STAGES, shards * tall, LANES), jnp.bfloat16),
                pltpu.VMEM((shards * tall, LANES), jnp.bfloat16),
                pltpu.VMEM((STAGES, shards * tall, LANES), jnp.bfloat16),
                pltpu.VMEM((shards * per_source, rows, LANES), jnp.float32),
                pltpu.VMEM((LMAX, pairs, 1, LANES), jnp.float32),
                pltpu.VMEM((shards, 1, LANES), jnp.int32),
                pltpu.VMEM((2 * shards, 1, LANES), jnp.int32),
                pltpu.VMEM((LMAX * KB, 1, LANES), jnp.int32),
                pltpu.SMEM((2 * shards, 1, LANES), jnp.int32),
                pltpu.SMEM((LMAX * KB, 1, LANES), jnp.int32),
                pltpu.SemaphoreType.DMA((4,)),
                pltpu.SemaphoreType.DMA((LMAX,)),
                pltpu.SemaphoreType.DMA,
                pltpu.SemaphoreType.DMA((shards,)),
                pltpu.SemaphoreType.DMA,
                pltpu.SemaphoreType.DMA((shards,)),
                pltpu.SemaphoreType.DMA,
                pltpu.SemaphoreType.DMA,
                pltpu.SemaphoreType.REGULAR,
                pltpu.SemaphoreType.DMA((STAGES,)),
                pltpu.SemaphoreType.DMA,
                pltpu.SemaphoreType.DMA((STAGES, shards)),
            ],
            compiler_params=pltpu.CompilerParams(
                collective_id=0, has_side_effects=True, vmem_limit_bytes=60 * 1024 * 1024
            ),
        )(depth, pending, arriving, coefficients, offsets, lookup)

    placed = (
        P("segment", None, "neuron"),
        P(None, None, "neuron"),
        P("segment", None, None, None, "neuron"),
        P("segment", None, "neuron"),
        P("segment", None, None, "neuron"),
        P("segment"),
    )
    return jax.shard_map(
        per_device,
        mesh=mesh,
        in_specs=placed,
        out_specs=P("segment", None, "neuron"),
        check_vma=False,
    )
```

```python
import functools

import jax
import jax.numpy as jnp
from jax import lax
from jax.experimental import pallas as pl
from jax.experimental.pallas import tpu as pltpu
from jax.sharding import PartitionSpec as P

BLK = 64
KB = 4
LMAX = 2
STAGES = 4
LANES = 128
SIDE = 4
MESH = pl.DeviceIdType.MESH


def torus_distance(step):
    return sum(min(c, SIDE - c) for c in step)


STEPS_FAR = sorted(
    ((dy, dx) for dy in range(SIDE) for dx in range(SIDE)), key=lambda s: -torus_distance(s)
)
STEPS_NEAR = sorted(
    ((dy, dx) for dy in range(SIDE) for dx in range(SIDE)), key=torus_distance
)


def lists_of_blocks(idx_ref, shards, per_source):
    rows = LMAX * KB
    per_shard = idx_ref.shape[-1]
    shard = lax.broadcasted_iota(jnp.int32, (shards, per_shard), 0)
    place = lax.broadcasted_iota(jnp.int32, (LANES, per_shard), 0)
    before = (
        lax.broadcasted_iota(jnp.int32, (per_shard, per_shard), 0)
        < lax.broadcasted_iota(jnp.int32, (per_shard, per_shard), 1)
    ).astype(jnp.bfloat16)
    entries = [idx_ref[0, r // KB, pl.ds(r % KB, 1), :] for r in range(rows)]
    sources = [e // per_shard for e in entries]
    masks = [(jnp.broadcast_to(s, shard.shape) == shard).astype(jnp.float32) for s in sources]
    ahead = jnp.dot(
        jnp.concatenate(masks, axis=0).astype(jnp.bfloat16),
        before,
        preferred_element_type=jnp.float32,
    )
    wanted = jnp.zeros((shards, LANES), jnp.float32)
    slots = []
    for level in range(LMAX):
        count = jnp.zeros((shards, 1), jnp.float32)
        for k in range(KB):
            r = level * KB + k
            mask = masks[r]
            rank = jnp.sum(
                mask * (ahead[r * shards : (r + 1) * shards] + count), axis=0, keepdims=True
            ).astype(jnp.int32)
            rank = jnp.clip(rank, 0, per_source - 1)
            side, pair = rank & 1, rank >> 1
            count = count + jnp.sum(mask, axis=1, keepdims=True)
            tile = sources[r] * (per_source // 2) + pair
            slots.append(tile + (side ^ (k & 1)) * (shards * per_source // 2))
            local = entries[r] & (per_shard - 1)
            local = ((local >> 1) + ((local ^ rank) & 1) * (per_shard // 2)).astype(jnp.float32)
            chosen = (mask * local).astype(jnp.bfloat16)
            placed = (
                jnp.broadcast_to(rank + level * per_source, place.shape) == place
            ).astype(jnp.bfloat16)
            wanted = wanted + lax.dot_general(
                chosen, placed, (((1,), (1,)), ((), ())), preferred_element_type=jnp.float32
            )
    return jnp.clip(wanted.astype(jnp.int32), 0, per_shard - 1), slots


def kernel(
    segments,
    shards,
    depth_ref,
    pending_ref,
    arriving_ref,
    weight_ref,
    offset_ref,
    idx_ref,
    out_ref,
    pending,
    arriving,
    offsets,
    idx,
    weights,
    own,
    entering,
    send,
    send_entering,
    recv,
    table,
    bias,
    wants,
    arrived,
    slot_vmem,
    lists,
    slots,
    load_sem,
    weight_sem,
    slot_sem,
    row_sem,
    list_send_sem,
    list_sem,
    next_send_sem,
    next_sem,
    next_here,
    send_sem,
    send_entering_sem,
    recv_sem,
):
    seg = lax.axis_index("segment")
    me = lax.axis_index("neuron")
    first, last = seg == 0, seg == segments - 1
    after = lax.rem(seg + 1, segments)
    ahead = lax.rem(seg + segments - 1, segments)
    row, col = lax.div(me, SIDE), lax.rem(me, SIDE)

    def peer(step):
        return lax.rem(row + step[0], SIDE) * SIDE + lax.rem(col + step[1], SIDE)

    far = [peer(s) for s in STEPS_FAR]
    near = [peer(s) for s in STEPS_NEAR]
    blocks = idx_ref.shape[-1]
    per_source = KB * blocks // shards
    tall = per_source * 4
    column_tiles = weights.shape[-1] // LANES
    pairs = column_tiles
    low = lax.broadcasted_iota(jnp.int32, (8, LANES), 1) < BLK

    load = [
        pltpu.make_async_copy(source, target, load_sem.at[i])
        for i, (source, target) in enumerate(
            ((idx_ref, idx), (pending_ref, pending), (offset_ref, offsets), (arriving_ref, arriving))
        )
    ]
    load[0].start()
    barrier = pltpu.get_barrier_semaphore()
    for p in far[:-1]:
        pl.semaphore_signal(barrier, inc=1, device_id=(seg, p), device_id_type=MESH)

    @pl.when(jnp.logical_not(last))
    def _():
        pl.semaphore_signal(barrier, inc=1, device_id=(after, me), device_id_type=MESH)

    for copy in load[1:]:
        copy.start()

    load[0].wait()
    wanted, landing = lists_of_blocks(idx, shards, per_source)
    for v in range(shards):
        wants[v] = wanted[v : v + 1]

    pl.semaphore_wait(barrier, jnp.where(first, shards - 1, shards))

    def list_copy(p):
        return pltpu.make_async_remote_copy(
            src_ref=wants.at[p],
            dst_ref=arrived.at[me],
            send_sem=list_send_sem,
            recv_sem=list_sem.at[me],
            device_id=(seg, p),
            device_id_type=MESH,
        )

    for p in far[:-1]:
        list_copy(p).start()
    pltpu.make_async_copy(wants.at[me], arrived.at[me], list_sem.at[me]).start()

    @pl.when(jnp.logical_not(first))
    def _():
        pl.semaphore_signal(next_here, inc=1, device_id=(ahead, me), device_id_type=MESH)

    for r in range(LMAX * KB):
        slot_vmem[r, :, pl.ds(0, blocks)] = landing[r]
    slot_copy = pltpu.make_async_copy(slot_vmem, slots, slot_sem)
    slot_copy.start()

    for level in range(LMAX):
        pltpu.make_async_copy(
            weight_ref.at[0, level], weights.at[level], weight_sem.at[level]
        ).start()

    def keep(tiles, where):
        tiles = tiles.reshape(pairs, 8, LANES)
        where[pl.ds(0, pairs)] = tiles
        where[pl.ds(pairs, pairs)] = pltpu.roll(tiles, BLK, 2)

    def tiles_of(ref):
        return jnp.concatenate(
            [ref[0, :, pl.ds(p * LANES, LANES)] for p in range(pairs)], axis=0
        ).astype(jnp.float32)

    load[1].wait()
    keep(tiles_of(pending), own)
    load[2].wait()
    for level in range(LMAX):
        for p in range(pairs):
            bias[level, p] = offsets[0, pl.ds(level, 1), pl.ds(p * LANES, LANES)]

    def row_copy(p):
        return pltpu.make_async_copy(arrived.at[p], lists.at[p], row_sem.at[p])

    def list_take(p):
        pltpu.make_async_copy(wants.at[p], arrived.at[p], list_sem.at[p]).wait()
        row_copy(p).start()

    def gather_for(where, level, row, target, p):
        at = level * per_source
        even, odd = (
            jnp.concatenate(
                [where[lists[row, 0, at + 2 * q + h]] for q in range(per_source // 2)], axis=0
            )
            for h in range(2)
        )
        side = jnp.concatenate([low] * (per_source // 2), axis=0)
        target[block_rows(p), :] = jnp.where(side, even, odd).astype(jnp.bfloat16)

    def block_rows(p):
        return pl.ds(pl.multiple_of(p * tall, tall), tall)

    def give(t, s, p, source, sem, local):
        if local:
            pltpu.make_async_copy(
                source.at[block_rows(p)], recv.at[t, block_rows(p)], recv_sem.at[t, me]
            ).start()
            return
        pltpu.make_async_remote_copy(
            src_ref=source.at[block_rows(p)],
            dst_ref=recv.at[t, block_rows(me)],
            send_sem=sem,
            recv_sem=recv_sem.at[t, me],
            device_id=(s, p),
            device_id_type=MESH,
        ).start()

    depth = depth_ref[0]

    def send_first():
        def one(i):
            row_copy(near[i]).wait()
            gather_for(own, 0, near[i], send.at[0], near[i])
            give(0, seg, near[i], send.at[0], send_sem.at[0], i == 0)

        for i in range(shards):
            list_take(near[i])
        for i in reversed(range(shards)):
            one(i)

        @pl.when(jnp.logical_not(first))
        def _():
            for p in far:
                pltpu.make_async_remote_copy(
                    src_ref=wants.at[p],
                    dst_ref=arrived.at[shards + me],
                    send_sem=next_send_sem,
                    recv_sem=next_sem,
                    device_id=(ahead, p),
                    device_id_type=MESH,
                ).start()

        load[3].wait()

        @pl.when(first)
        def _():
            keep(tiles_of(arriving), entering)
            for i, p in enumerate(far):
                gather_for(entering, 0, p, send_entering, p)
                give(2, seg, p, send_entering, send_entering_sem, i == shards - 1)

        slot_copy.wait()

    def send_within(t):
        for i, p in enumerate(far):
            gather_for(own, t % LMAX, p, send.at[t], p)
            give(t, seg, p, send.at[t], send_sem.at[t], i == shards - 1)

    def take_next_lists():
        later = pl.ds(shards, shards)

        @pl.when(jnp.logical_not(last))
        def _():
            pltpu.make_async_copy(wants, arrived.at[later], next_sem).wait()
            every = pltpu.make_async_copy(arrived.at[later], lists.at[later], slot_sem)
            every.start()
            pl.semaphore_wait(next_here, 1)
            every.wait()

    def send_across(t):
        @pl.when(jnp.logical_not(last))
        def _():
            for p in far:
                gather_for(own, 0, shards + p, send.at[t], p)
                give(t, after, p, send.at[t], send_sem.at[t], False)

    def apply(t):
        level = t % LMAX
        if t < LMAX:
            pltpu.make_async_copy(
                weight_ref.at[0, level], weight_ref.at[0, level], weight_sem.at[level]
            ).wait()
        half = shards * per_source // 2
        deep = per_source // 2
        for v in near:
            pltpu.make_async_copy(
                send.at[t, block_rows(v)], recv.at[t, block_rows(v)], recv_sem.at[t, v]
            ).wait()
        for v in near:
            got = recv[t, block_rows(v), :].astype(jnp.float32).reshape(deep, 8, LANES)
            table[pl.ds(v * deep, deep)] = got
            table[pl.ds(half + v * deep, deep)] = pltpu.roll(got, BLK, 2)
        side = jnp.concatenate([low] * 4, axis=0)
        fresh = []
        for c in range(column_tiles // 2):
            left = []
            for pair in range(KB // 2):
                a, b = (
                    jnp.concatenate(
                        [table[slots[level * KB + 2 * pair + h, 0, 4 * c + j]] for j in range(4)], axis=0
                    )
                    for h in range(2)
                )
                left.append(jnp.where(side, a, b))
            left = jnp.concatenate(left, axis=1).astype(jnp.bfloat16)
            right = weights[level, :, :, pl.ds(2 * c * LANES, 2 * LANES)]
            right = right.reshape(KB * BLK, 2 * LANES)
            total = jnp.dot(left, right, preferred_element_type=jnp.float32)
            fresh.append(jnp.where(low, total[0:8, 0:LANES], total[8:16, 0:LANES]))
            fresh.append(jnp.where(low, total[16:24, LANES:], total[24:32, LANES:]))
        fresh = jnp.concatenate(fresh, axis=0).reshape(pairs, 8, LANES) + bias[level]
        fresh = jnp.clip(fresh, 0.0, 32.0).astype(jnp.bfloat16).astype(jnp.float32)
        if level > 0:
            fresh = jnp.where(depth > level, fresh, own[pl.ds(0, pairs)])
        if t < STAGES - 1:
            keep(fresh, own)
        else:
            for p in range(pairs):
                out_ref[0, :, pl.ds(p * LANES, LANES)] = fresh[p].astype(jnp.bfloat16)

    send_first()
    apply(0)
    send_within(1)
    take_next_lists()
    apply(1)
    send_across(2)
    apply(2)
    send_within(3)
    apply(3)

    def settle(rows, sem):
        pltpu.make_async_copy(send.at[0, rows], recv.at[0, rows], sem).wait()

    some, whole = pl.ds(0, (shards - 1) * tall), pl.ds(0, shards * tall)
    for t in (0, 1, 3):
        settle(some, send_sem.at[t])

    @pl.when(jnp.logical_not(last))
    def _():
        settle(whole, send_sem.at[2])

    @pl.when(first)
    def _():
        settle(some, send_entering_sem)

    pltpu.make_async_copy(
        wants.at[pl.ds(0, shards - 1)], arrived.at[pl.ds(0, shards - 1)], list_send_sem
    ).wait()

    @pl.when(jnp.logical_not(first))
    def _():
        pltpu.make_async_copy(wants, arrived.at[pl.ds(0, shards)], next_send_sem).wait()


def solution(mesh):
    segments, shards = mesh.shape["segment"], mesh.shape["neuron"]

    def per_device(pending, arriving, coefficients, offsets, lookup, depth):
        rows, wide = pending.shape[1:]
        blocks = lookup.shape[-1]
        per_source = KB * blocks // shards
        tall = per_source * 4
        pairs = wide // LANES
        anywhere = pl.BlockSpec(memory_space=pl.ANY)
        return pl.pallas_call(
            functools.partial(kernel, segments, shards),
            out_shape=jax.ShapeDtypeStruct(pending.shape, jnp.bfloat16),
            in_specs=[pl.BlockSpec(memory_space=pltpu.SMEM)] + [anywhere] * 5,
            out_specs=pl.BlockSpec(memory_space=pltpu.VMEM),
            scratch_shapes=[
                pltpu.VMEM(pending.shape, jnp.bfloat16),
                pltpu.VMEM(arriving.shape, jnp.bfloat16),
                pltpu.VMEM(offsets.shape, jnp.float32),
                pltpu.VMEM(lookup.shape, jnp.int32),
                pltpu.VMEM((LMAX, KB, BLK, wide), jnp.bfloat16),
                pltpu.VMEM((blocks, rows, LANES), jnp.float32),
                pltpu.VMEM((blocks, rows, LANES), jnp.float32),
                pltpu.VMEM((STAGES, shards * tall, LANES), jnp.bfloat16),
                pltpu.VMEM((shards * tall, LANES), jnp.bfloat16),
                pltpu.VMEM((STAGES, shards * tall, LANES), jnp.bfloat16),
                pltpu.VMEM((shards * per_source, rows, LANES), jnp.float32),
                pltpu.VMEM((LMAX, pairs, 1, LANES), jnp.float32),
                pltpu.VMEM((shards, 1, LANES), jnp.int32),
                pltpu.VMEM((2 * shards, 1, LANES), jnp.int32),
                pltpu.VMEM((LMAX * KB, 1, LANES), jnp.int32),
                pltpu.SMEM((2 * shards, 1, LANES), jnp.int32),
                pltpu.SMEM((LMAX * KB, 1, LANES), jnp.int32),
                pltpu.SemaphoreType.DMA((4,)),
                pltpu.SemaphoreType.DMA((LMAX,)),
                pltpu.SemaphoreType.DMA,
                pltpu.SemaphoreType.DMA((shards,)),
                pltpu.SemaphoreType.DMA,
                pltpu.SemaphoreType.DMA((shards,)),
                pltpu.SemaphoreType.DMA,
                pltpu.SemaphoreType.DMA,
                pltpu.SemaphoreType.REGULAR,
                pltpu.SemaphoreType.DMA((STAGES,)),
                pltpu.SemaphoreType.DMA,
                pltpu.SemaphoreType.DMA((STAGES, shards)),
            ],
            compiler_params=pltpu.CompilerParams(
                collective_id=0, has_side_effects=True, vmem_limit_bytes=60 * 1024 * 1024
            ),
        )(depth, pending, arriving, coefficients, offsets, lookup)

    placed = (
        P("segment", None, "neuron"),
        P(None, None, "neuron"),
        P("segment", None, None, None, "neuron"),
        P("segment", None, "neuron"),
        P("segment", None, None, "neuron"),
        P("segment"),
    )
    return jax.shard_map(
        per_device,
        mesh=mesh,
        in_specs=placed,
        out_specs=P("segment", None, "neuron"),
        check_vma=False,
    )
```
